256 devices in a mesh: dp: 8 (over x, core), seq: 32 (over z, y).
Axes of the slice: x: 4, y: 4, z: 8, core: 2. Of those that a mesh axis runs over, the one named last changes fastest.
Arguments:
- queries: bfloat16 [8, 32, 256, 1536], P('dp', 'seq'), may hold values from -6 to 6
- keys_spatial: bfloat16 [8, 32, 256, 1536], P('dp', 'seq'), may hold values from -6 to 6
- values_spatial: bfloat16 [8, 32, 256, 1536], P('dp', 'seq'), may hold values from -6 to 6
- temporal_keys: bfloat16 [8, 32, 256, 1536], P('dp', 'seq'), may hold values from -6 to 6
- temporal_values: bfloat16 [8, 32, 256, 1536], P('dp', 'seq'), may hold values from -6 to 6
- tile_mask: int32 [8, 32, 2, 2], P('dp', 'seq'), may hold values 0 or 1
- query_weight: bfloat16 [1536, 1536], P('seq'), may hold values from -0.15625 to 0.15625
- out_grad: bfloat16 [8, 32, 256, 1536], P('dp', None, 'seq'), may hold values from -6 to 6
Outputs:
- d_queries: bfloat16 [8, 32, 256, 1536], P('dp', 'seq')
- d_keys_spatial: bfloat16 [8, 32, 256, 1536], P('dp', 'seq')
- d_values_spatial: bfloat16 [8, 32, 256, 1536], P('dp', 'seq')
- d_temporal_keys: bfloat16 [8, 32, 256, 1536], P('dp', 'seq')
- d_temporal_values: bfloat16 [8, 32, 256, 1536], P('dp', 'seq')
- d_weight: bfloat16 [1536, 1536], P('seq')
The draws below stay inside these ranges and needn't reach their ends.
All inputs are finite; a program needn't handle non-finite values. No bound on the sum of `tile_mask` on one device may be relied on, other than what follows from the above.
Results may differ from the reference program's by a relative error of at most 0.03.
Values may be sent and summed in bfloat16 or wider, within the bound.
A program may use at most 192 MiB of HBM per device.

```python
import math
import jax
import jax.numpy as jnp
from jax import lax

HEADS = 12
HEAD_DIM = 128
TILE = 128
PATCH = 256
WIDTH = 1536
TILES = 2
FRAMES = 32
CLIPS = 8


def with_ends(values, stream_key, low, high):
    index_at = [jax.random.randint(jax.random.fold_in(stream_key, axis), (), 0, length) for axis, length in enumerate(values.shape)]
    main_axis = values.shape.index(max(values.shape))
    beside = index_at[:main_axis] + [(index_at[main_axis] + 1) % values.shape[main_axis]] + index_at[main_axis + 1:]
    return values.at[tuple(index_at)].set(low).at[tuple(beside)].set(high)


def level_of(stream_key, extent, pieces, low, high):
    loudness = 1.0
    for position, shards_of in pieces:
        draws = jax.random.uniform(jax.random.fold_in(jax.random.fold_in(stream_key, 6), position), (shards_of,), jnp.float32, low / len(pieces), high / len(pieces))
        loudness = loudness * jnp.repeat(jnp.exp(draws), extent[position] // shards_of).reshape((-1,) + (1,) * (len(extent) - 1 - position))
    return loudness


def gaussian(key, extent, scale, limit, pieces=(), kind=jnp.bfloat16):
    entries = jax.random.normal(key, extent, jnp.float32) * scale
    if len(pieces) > 0:
        entries = level_of(key, extent, pieces, -0.22, 0.18) * entries
    return jnp.clip(entries, min=-limit, max=limit).astype(kind)


def setup_inputs(seed: int = 0) -> dict:
    key_of = jax.random.split(jax.random.key(seed), 9)
    queries = gaussian(key_of[0], (CLIPS, FRAMES, PATCH, WIDTH), 1.0, 6.0, ((0, 8), (1, 32)))
    keys_spatial = gaussian(key_of[1], (CLIPS, FRAMES, PATCH, WIDTH), 1.0, 6.0, ((0, 8), (1, 32)))
    values_spatial = gaussian(key_of[2], (CLIPS, FRAMES, PATCH, WIDTH), 1.0, 6.0, ((0, 8), (1, 32)))
    temporal_keys = gaussian(key_of[3], (CLIPS, FRAMES, PATCH, WIDTH), 1.0, 6.0, ((0, 8), (1, 32)))
    temporal_values = gaussian(key_of[4], (CLIPS, FRAMES, PATCH, WIDTH), 1.0, 6.0, ((0, 8), (1, 32)))
    tile_mask = with_ends((jax.random.randint(key_of[5], (CLIPS, FRAMES, TILES, TILES), 0, 2) < 1).astype(jnp.int32), jax.random.fold_in(key_of[5], 1), 0, 1)
    query_weight = gaussian(key_of[6], (WIDTH, WIDTH), WIDTH ** -0.5, 0.15625, ((0, 32),))
    out_grad = gaussian(key_of[7], (CLIPS, FRAMES, PATCH, WIDTH), 1.0, 6.0, ((0, 8), (2, 32)))
    return dict(queries=queries, keys_spatial=keys_spatial, values_spatial=values_spatial, temporal_keys=temporal_keys, temporal_values=temporal_values, tile_mask=tile_mask, query_weight=query_weight, out_grad=out_grad)


def head_rmsnorm(values_in):
    floats = values_in.astype(jnp.float32)
    floats = floats.reshape(floats.shape[:-1] + (HEADS, HEAD_DIM))
    scaled = floats * lax.rsqrt(lax.optimization_barrier(jnp.mean(floats * floats, axis=-1, keepdims=True)) + 1e-06)
    return scaled.astype(jnp.bfloat16)

def spatial_frame(queries, keys_in, values_in, allowed):
    patches = queries.shape[0]
    query_norm = head_rmsnorm(queries).astype(jnp.float32)
    key_norm = head_rmsnorm(keys_in).astype(jnp.float32)
    value_heads = values_in.reshape(patches, HEADS, HEAD_DIM).astype(jnp.float32)
    scores = jnp.einsum('phd,khd->hpk', query_norm, key_norm) / math.sqrt(HEAD_DIM)
    full_mask = jnp.repeat(jnp.repeat(allowed, TILE, axis=0), TILE, axis=1)
    exps = jnp.exp(scores) * full_mask[None]
    weights = (exps / lax.optimization_barrier(jnp.sum(exps, axis=-1, keepdims=True))).astype(jnp.bfloat16)
    result = jnp.einsum('hpk,khd->phd', weights.astype(jnp.float32), value_heads)
    return result.astype(jnp.bfloat16).reshape(patches, HEADS * HEAD_DIM)

def temporal_block(projected, keys_in, values_in):
    dims_in = projected.shape
    query_norm = head_rmsnorm(projected).astype(jnp.float32)
    key_norm = head_rmsnorm(keys_in).astype(jnp.float32)
    value_heads = values_in.reshape(dims_in[:-1] + (HEADS, HEAD_DIM)).astype(jnp.float32)
    scores = jnp.einsum('cfphd,cgphd->cphfg', query_norm, key_norm) / math.sqrt(HEAD_DIM)
    exps = jnp.exp(scores)
    weights = (exps / lax.optimization_barrier(jnp.sum(exps, axis=-1, keepdims=True))).astype(jnp.bfloat16)
    result = jnp.einsum('cphfg,cgphd->cfphd', weights.astype(jnp.float32), value_heads)
    return result.astype(jnp.bfloat16).reshape(dims_in)

def reference(queries, keys_spatial, values_spatial, temporal_keys, temporal_values, tile_mask, query_weight, out_grad):
    clip_count, frame_count, patches, width = queries.shape
    tile_count = patches // TILE
    diagonal = jnp.eye(tile_count, dtype=bool)
    allowed = jnp.logical_or(tile_mask == 1, diagonal).astype(jnp.float32)
    allowed = allowed.reshape(clip_count * frame_count, tile_count, tile_count)

    def flatten(array_in):
        return array_in.reshape(clip_count * frame_count, patches, width)

    def forward_frame(inputs):
        return spatial_frame(inputs[0], inputs[1], inputs[2], inputs[3])
    spatial_out = lax.map(forward_frame, (flatten(queries), flatten(keys_spatial), flatten(values_spatial), allowed))
    spatial_rows = spatial_out.reshape(-1, width)
    projected = jnp.dot(spatial_rows, query_weight, preferred_element_type=jnp.float32).astype(jnp.bfloat16)
    projected = projected.reshape(clip_count, frame_count, patches, width)
    temporal_out, temporal_back = jax.vjp(temporal_block, projected, temporal_keys, temporal_values)
    d_projected, d_temporal_keys, d_temporal_values = temporal_back(out_grad)
    d_rows = d_projected.reshape(-1, width)
    d_weight = lax.dot_general(spatial_rows, d_rows, (((0,), (0,)), ((), ())), preferred_element_type=jnp.float32).astype(jnp.bfloat16)
    d_spatial = lax.dot_general(d_rows, query_weight, (((1,), (1,)), ((), ())), preferred_element_type=jnp.float32).astype(jnp.bfloat16)
    d_spatial = d_spatial.reshape(clip_count * frame_count, patches, width)

    def backward_frame(inputs):
        mask_here = inputs[3]

        def frame_fn(first_in, second_in, third_in):
            return spatial_frame(first_in, second_in, third_in, mask_here)
        unused_out, frame_back = jax.vjp(frame_fn, inputs[0], inputs[1], inputs[2])
        return frame_back(inputs[4])
    d_queries, d_keys, d_values = lax.map(backward_frame, (flatten(queries), flatten(keys_spatial), flatten(values_spatial), allowed, d_spatial))
    whole = (clip_count, frame_count, patches, width)
    return (d_queries.reshape(whole), d_keys.reshape(whole), d_values.reshape(whole), d_temporal_keys, d_temporal_values, d_weight)
```

```python
import math

import jax
import jax.numpy as jnp
from jax import lax
from jax.experimental import pallas as pl
from jax.experimental.pallas import tpu as pltpu
from jax.sharding import PartitionSpec as P

HEADS = 12
HEAD_DIM = 128
TILE = 128
WIDTH = HEADS * HEAD_DIM
NX, NY, NZ = 4, 4, 8
SEQ = NZ * NY
ROWS = 48
PATCH = 256
PAIR = 2 * HEAD_DIM
PAIRS = WIDTH // PAIR
CHUNK = 512
THIRDS = WIDTH // CHUNK
COLS = WIDTH // NX
SCALE = 1.0 / math.sqrt(HEAD_DIM)
SCALE2 = SCALE * math.log2(math.e)
EPS = 1e-06
MESH = pl.DeviceIdType.MESH
F32 = jnp.float32
BF16 = jnp.bfloat16


def dot(a, b, contract):
    return lax.dot_general(a, b, ((contract[:1], contract[1:]), ((), ())), preferred_element_type=F32)


def inverse_rms(a):
    return lax.rsqrt(jnp.mean(a * a, axis=-1, keepdims=True) + EPS)


def norm_back(grad, normed, inverse):
    return (inverse * SCALE) * (grad - normed * jnp.mean(grad * normed, axis=-1, keepdims=True))


def softmax(q_norm, k_norm, mask):
    exps = jnp.exp2(dot(q_norm, k_norm, (1, 1)) * SCALE2) * mask
    return exps * (1.0 / jnp.sum(exps, axis=-1, keepdims=True))


def attention_back(weights, weights_b, q, k, qn, kn, rq, rk, qn_b, kn_b, v, grad):
    d_weights = dot(grad, v, (1, 1))
    delta = jnp.sum(weights * d_weights, axis=-1, keepdims=True)
    d_scores = (weights * (d_weights - delta)).astype(BF16)
    d_v = dot(weights_b, grad, (0, 0))
    d_q = norm_back(dot(d_scores, kn_b, (1, 0)), qn, rq)
    d_k = norm_back(dot(d_scores, qn_b, (0, 0)), kn, rk)
    return d_q, d_k, d_v


def wait_for(ref, sem):
    pltpu.make_async_copy(ref, ref, sem).wait()


def kernel(
    tile_ref, q_ref, k_ref, v_ref, tk_ref, tv_ref, w_ref, og_ref,
    dq_ref, dk_ref, dv_ref, dtk_ref, dtv_ref, dw_ref,
    weight, mask, tmask, spatial, k_buf, v_buf, s_buf, s_mat, d_mat, attn,
    dk_send, dv_send, ds_send, ds_buf,
    part, core_in, x_in, x_sum, y_in, y_sum, z_in, final,
    send, a2a_in, w_in, wx_in, core_sem, x_sem, y_sem, z_sem, out_sem, g_send, local,
):
    d = lax.axis_index("dp")
    s = lax.axis_index("seq")
    x, c = d // 2, d % 2
    z, y = s // NY, s % NY
    sibling = {"dp": x * 2 + 1 - c}
    active = y % 2 == c
    idle = y % 2 != c

    def seq_peer(o):
        return lax.rem(s + o, SEQ)

    def x_peer(o):
        return {"dp": lax.rem(x + o, NX) * 2 + c}

    def y_peer(o):
        return {"seq": z * NY + lax.rem(y + o, NY)}

    def z_peer(o):
        return {"seq": lax.rem(z + o, NZ) * NY + y}

    def remote(src, dst, send_sem, recv_sem, device):
        pltpu.make_async_remote_copy(
            src, dst, send_sem, recv_sem, device_id=device, device_id_type=MESH
        ).start()

    def exchange(src, dst, lanes, send_sem, recv_sem):
        pltpu.make_async_copy(src.at[s, :, lanes], dst.at[s, :, lanes], recv_sem).start()

        @pl.loop(1, SEQ)
        def _(o):
            j = seq_peer(o)
            remote(src.at[j, :, lanes], dst.at[s, :, lanes], send_sem, recv_sem, {"seq": j})

    def lanes_of(n, width):
        return pl.ds(pl.multiple_of(n * width, width), width)

    all_lanes = pl.ds(0, WIDTH)
    own_cols = lanes_of(x, COLS)

    weight[z, y] = w_ref[...]

    barrier = pltpu.get_barrier_semaphore()

    @pl.loop(1, SEQ)
    def _(o):
        pl.semaphore_signal(barrier, inc=1, device_id={"seq": seq_peer(o)}, device_id_type=MESH)

    @pl.loop(1, 2 * NX)
    def _(o):
        pl.semaphore_signal(barrier, inc=1, device_id={"dp": lax.rem(d + o, 2 * NX)}, device_id_type=MESH)

    pl.semaphore_wait(barrier, SEQ - 1 + 2 * NX - 1)

    @pl.when(active)
    def _():
        src = weight.at[z, y, :, own_cols]

        @pl.loop(1, NZ)
        def _(o):
            remote(src, src, send.at[0], w_in.at[0], z_peer(o))

    exchange(tk_ref, k_buf, all_lanes, send.at[1], a2a_in.at[0])

    ones = jnp.ones((TILE, TILE), F32)
    for a in range(2):
        for b in range(2):
            value = 1.0 if a == b else jnp.where(tile_ref[a, b] == 1, 1.0, 0.0).astype(F32)
            mask[a * TILE:(a + 1) * TILE, b * TILE:(b + 1) * TILE] = ones * value
    row = lax.broadcasted_iota(jnp.int32, (PATCH, PATCH), 0)
    col = lax.broadcasted_iota(jnp.int32, (PATCH, PATCH), 1)
    tmask[...] = jnp.where(row % 8 == col % 8, 1.0, 0.0).astype(F32)

    @pl.loop(0, PAIRS)
    def _(n):
        lanes = lanes_of(n, PAIR)
        q2, k2 = q_ref[:, lanes].astype(F32), k_ref[:, lanes].astype(F32)
        v2 = v_ref[:, lanes]
        outs = []
        for h in range(2):
            cut = slice(h * HEAD_DIM, (h + 1) * HEAD_DIM)
            q, k = q2[:, cut], k2[:, cut]
            qn = (q * inverse_rms(q)).astype(BF16)
            kn = (k * inverse_rms(k)).astype(BF16)
            weights = softmax(qn, kn, mask[...]).astype(BF16)
            attn[2 * n + h] = weights
            outs.append(dot(weights, v2[:, cut], (1, 0)))
        out = jnp.concatenate(outs, axis=1)
        spatial[:, :, lanes] = out.reshape(SEQ, 8, PAIR).astype(BF16)

        @pl.when(n % 2 == 1)
        def _():
            exchange(spatial, s_buf, lanes_of(n // 2, CHUNK), send.at[2], a2a_in.at[1])

        @pl.when(n == 1)
        def _():
            @pl.when(active)
            def _():
                wait_for(weight.at[pl.ds(0, NZ - 1), y, :, own_cols], w_in.at[0])
                src = weight.at[:, y, :, own_cols]

                @pl.loop(1, NY)
                def _(o):
                    remote(src, src, send.at[3], w_in.at[1], y_peer(o))

        @pl.when(n == 4)
        def _():
            @pl.when(active)
            def _():
                wait_for(weight.at[:, 0, :, own_cols], w_in.at[1])

            @pl.when(idle)
            def _():
                wait_for(weight.at[:, pl.ds(0, 2), :, own_cols], w_in.at[1])

            for h in range(2):
                src = weight.at[:, c + 2 * h, :, own_cols]

                @pl.loop(1, NX)
                def _(o):
                    remote(src, src, send.at[4], wx_in.at[o - 1], x_peer(o))

                remote(src, src, send.at[5], w_in.at[2], sibling)

    exchange(tv_ref, v_buf, all_lanes, send.at[6], a2a_in.at[2])

    for o in (1, 3, 2):
        cols = lanes_of(lax.rem(x + NX - o, NX), COLS)
        wait_for(weight.at[:, pl.ds(0, 2), :, cols], wx_in.at[o - 1])
        for h in range(2):
            src = weight.at[:, c + 2 * h, :, cols]
            remote(src, src, send.at[5], w_in.at[2], sibling)

    wait_for(s_buf, a2a_in.at[1])
    for n in range(PAIRS):
        lanes = slice(n * PAIR, (n + 1) * PAIR)
        s_mat[:, lanes] = s_buf[:, :, lanes].astype(F32).reshape(PATCH, PAIR).astype(BF16)
    wait_for(weight.at[:, pl.ds(0, 2)], w_in.at[2])
    wait_for(k_buf, a2a_in.at[0])
    wait_for(v_buf, a2a_in.at[2])

    @pl.loop(0, PAIRS)
    def _(n):
        lanes = lanes_of(n, PAIR)
        rows = weight[:, :, :, lanes].reshape(WIDTH, PAIR)
        q2 = dot(s_mat[...], rows, (1, 0)).astype(BF16).astype(F32)
        k2 = k_buf[:, :, lanes].astype(F32).reshape(PATCH, PAIR)
        v2 = v_buf[:, :, lanes].astype(F32).reshape(PATCH, PAIR).astype(BF16)
        g2 = og_ref[:, :, lanes].astype(F32).reshape(PATCH, PAIR).astype(BF16)
        d_qs, d_ks, d_vs = [], [], []
        for h in range(2):
            cut = slice(h * HEAD_DIM, (h + 1) * HEAD_DIM)
            q, k = q2[:, cut], k2[:, cut]
            rq, rk = inverse_rms(q), inverse_rms(k)
            qn, kn = q * rq, k * rk
            qn_b, kn_b = qn.astype(BF16), kn.astype(BF16)
            weights = softmax(qn_b, kn_b, tmask[...])
            d_q, d_k, d_v = attention_back(
                weights, weights.astype(BF16), q, k, qn, kn, rq, rk, qn_b, kn_b, v2[:, cut], g2[:, cut]
            )
            d_qs.append(d_q)
            d_ks.append(d_k)
            d_vs.append(d_v)
        d_mat[:, lanes] = jnp.concatenate(d_qs, axis=1).astype(BF16)
        dk_send[:, :, lanes] = jnp.concatenate(d_ks, axis=1).reshape(SEQ, 8, PAIR).astype(BF16)
        dv_send[:, :, lanes] = jnp.concatenate(d_vs, axis=1).reshape(SEQ, 8, PAIR).astype(BF16)

        @pl.when(n == 1)
        def _():
            first = pl.ds(0, CHUNK)
            exchange(dk_send, dtk_ref, first, send.at[7], a2a_in.at[3])
            exchange(dv_send, dtv_ref, first, send.at[8], a2a_in.at[4])

    @pl.loop(0, NZ // 2)
    def _(m):
        rows = weight[pl.ds(2 * m, 2)].reshape(2 * NY * ROWS, WIDTH)
        out = dot(d_mat[...], rows, (1, 1))
        lanes = lanes_of(m, 2 * NY * ROWS)
        ds_send[:, :, lanes] = out.reshape(SEQ, 8, 2 * NY * ROWS).astype(BF16)
        exchange(ds_send, ds_buf, lanes, send.at[9], a2a_in.at[5])

    rest = pl.ds(CHUNK, WIDTH - CHUNK)
    exchange(dk_send, dtk_ref, rest, send.at[7], a2a_in.at[3])
    exchange(dv_send, dtv_ref, rest, send.at[8], a2a_in.at[4])

    @pl.loop(0, THIRDS)
    def _(g):
        cols = d_mat[:, lanes_of(g, CHUNK)]

        @pl.loop(0, NZ // 2)
        def _(m):
            block = dot(s_mat[:, lanes_of(m, 2 * NY * ROWS)], cols, (0, 0))
            part[g, pl.ds(2 * m, 2)] = block.reshape(2, NY, ROWS, CHUNK).astype(BF16)

        for h in range(2):
            remote(part.at[g, :, 1 - c + 2 * h], core_in.at[g, h], g_send.at[0], core_sem.at[g], sibling)

    def x_step(g):
        wait_for(core_in.at[g], core_sem.at[g])
        for h in range(2):
            own = part[g, :, c + 2 * h].astype(F32) + core_in[g, h].astype(F32)
            part[g, :, c + 2 * h] = own.astype(BF16)

            @pl.loop(1, NX)
            def _(o):
                to = lax.rem(x + o, NX)
                remote(
                    part.at[g, :, c + 2 * h, :, lanes_of(to, HEAD_DIM)], x_in.at[g, o - 1, h],
                    g_send.at[1], x_sem.at[g], x_peer(o),
                )

    def y_step(g):
        wait_for(x_in.at[g], x_sem.at[g])
        for h in range(2):
            total = part[g, :, c + 2 * h, :, lanes_of(x, HEAD_DIM)].astype(F32)
            for o in range(NX - 1):
                total = total + x_in[g, o, h].astype(F32)
            x_sum[g, h] = total.astype(BF16)
            owner = c + 2 * h

            @pl.when(y != owner)
            def _():
                away = lax.rem(y - owner + NY, NY)
                remote(x_sum.at[g, h], y_in.at[g, away - 1], g_send.at[2], y_sem.at[g], {"seq": z * NY + owner})

    def z_step(g):
        @pl.when(active)
        def _():
            wait_for(y_in.at[g], y_sem.at[g])
            total = x_sum[g, y // 2].astype(F32)
            for o in range(NY - 1):
                total = total + y_in[g, o].astype(F32)
            y_sum[g] = total.astype(BF16)

            @pl.loop(1, NZ)
            def _(o):
                remote(
                    y_sum.at[g, lax.rem(z + o, NZ)], z_in.at[g, o - 1], g_send.at[3], z_sem.at[g], z_peer(o)
                )

    def out_step(g):
        @pl.when(active)
        def _():
            wait_for(z_in.at[g], z_sem.at[g])
            total = y_sum[g, z].astype(F32)
            for o in range(NZ - 1):
                total = total + z_in[g, o].astype(F32)
            final[g] = total.astype(BF16)
            dst = dw_ref.at[:, pl.ds(pl.multiple_of(g * CHUNK + x * HEAD_DIM, HEAD_DIM), HEAD_DIM)]
            pltpu.make_async_copy(final.at[g], dst, out_sem).start()

            @pl.loop(1, 2 * NX)
            def _(o):
                remote(final.at[g], dst, g_send.at[4], out_sem, {"dp": lax.rem(d + o, 2 * NX)})

    for g in range(THIRDS):
        x_step(g)
    y_step(0)
    y_step(1)

    wait_for(ds_buf, a2a_in.at[5])

    @pl.loop(0, PAIRS)
    def _(n):
        lanes = lanes_of(n, PAIR)
        q2, k2 = q_ref[:, lanes].astype(F32), k_ref[:, lanes].astype(F32)
        v2 = v_ref[:, lanes]
        g2 = ds_buf[:, :, lanes].astype(F32).reshape(PATCH, PAIR).astype(BF16)
        d_qs, d_ks, d_vs = [], [], []
        for h in range(2):
            cut = slice(h * HEAD_DIM, (h + 1) * HEAD_DIM)
            q, k = q2[:, cut], k2[:, cut]
            rq, rk = inverse_rms(q), inverse_rms(k)
            qn, kn = q * rq, k * rk
            weights = attn[2 * n + h]
            d_q, d_k, d_v = attention_back(
                weights.astype(F32), weights, q, k, qn, kn, rq, rk, qn.astype(BF16), kn.astype(BF16),
                v2[:, cut], g2[:, cut],
            )
            d_qs.append(d_q)
            d_ks.append(d_k)
            d_vs.append(d_v)
        dq_ref[:, lanes] = jnp.concatenate(d_qs, axis=1).astype(BF16)
        dk_ref[:, lanes] = jnp.concatenate(d_ks, axis=1).astype(BF16)
        dv_ref[:, lanes] = jnp.concatenate(d_vs, axis=1).astype(BF16)

        @pl.when(n == 1)
        def _():
            z_step(0)
            z_step(1)
            y_step(2)

        @pl.when(n == 4)
        def _():
            out_step(0)
            out_step(1)
            z_step(2)

    out_step(2)

    wait_for(dtk_ref, a2a_in.at[3])
    wait_for(dtv_ref, a2a_in.at[4])

    @pl.when(active)
    def _():
        wait_for(dw_ref, out_sem)

    @pl.when(idle)
    def _():
        wait_for(dw_ref, out_sem)

    sent = pl.ds(0, SEQ - 1)
    for i, buf in ((1, k_buf), (2, s_buf), (6, v_buf), (7, k_buf), (8, v_buf), (9, ds_buf)):
        wait_for(buf.at[sent], send.at[i])
    wait_for(weight.at[:, pl.ds(0, 2), :, pl.ds(0, 3 * COLS)], send.at[4])
    wait_for(weight.at[:, pl.ds(0, 2)], send.at[5])
    wait_for(core_in, g_send.at[0])
    wait_for(x_in, g_send.at[1])

    @pl.when(active)
    def _():
        wait_for(weight.at[pl.ds(0, NZ - 1), y, :, own_cols], send.at[0])
        wait_for(weight.at[:, 0, :, pl.ds(0, 3 * COLS)], send.at[3])
        wait_for(x_sum.at[:, 0], g_send.at[2])
        wait_for(z_in, g_send.at[3])
        wait_for(z_in, g_send.at[4])

    @pl.when(idle)
    def _():
        wait_for(x_sum, g_send.at[2])


def per_device(
    queries, keys_spatial, values_spatial, temporal_keys, temporal_values, tile_mask, query_weight, out_grad
):
    frame = (PATCH, WIDTH)
    blocks = (SEQ, 8, WIDTH)
    vmem = pl.BlockSpec(memory_space=pltpu.VMEM)
    smem = pl.BlockSpec(memory_space=pltpu.SMEM)
    anywhere = pl.BlockSpec(memory_space=pl.ANY)
    dma = pltpu.SemaphoreType.DMA

    def buf(*shape, kind=BF16):
        return pltpu.VMEM(shape, kind)

    d_q, d_k, d_v, d_tk, d_tv, d_w = pl.pallas_call(
        kernel,
        out_shape=(
            *(jax.ShapeDtypeStruct(frame, BF16) for _ in range(3)),
            *(jax.ShapeDtypeStruct(blocks, BF16) for _ in range(2)),
            jax.ShapeDtypeStruct((ROWS, WIDTH), BF16),
        ),
        in_specs=[smem, vmem, vmem, vmem, anywhere, anywhere, vmem, vmem],
        out_specs=(vmem, vmem, vmem, anywhere, anywhere, anywhere),
        scratch_shapes=[
            buf(NZ, NY, ROWS, WIDTH),
            buf(PATCH, PATCH, kind=F32),
            buf(PATCH, PATCH, kind=F32),
            buf(*blocks), buf(*blocks), buf(*blocks), buf(*blocks),
            buf(*frame), buf(*frame),
            buf(HEADS, PATCH, PATCH),
            buf(*blocks), buf(*blocks), buf(*blocks), buf(*blocks),
            buf(THIRDS, NZ, NY, ROWS, CHUNK),
            buf(THIRDS, 2, NZ, ROWS, CHUNK),
            buf(THIRDS, NX - 1, 2, NZ, ROWS, HEAD_DIM),
            buf(THIRDS, 2, NZ, ROWS, HEAD_DIM),
            buf(THIRDS, NY - 1, NZ, ROWS, HEAD_DIM),
            buf(THIRDS, NZ, ROWS, HEAD_DIM),
            buf(THIRDS, NZ - 1, ROWS, HEAD_DIM),
            buf(THIRDS, ROWS, HEAD_DIM),
            dma((10,)), dma((6,)), dma((3,)), dma((NX - 1,)),
            dma((THIRDS,)), dma((THIRDS,)), dma((THIRDS,)), dma((THIRDS,)), dma, dma((5,)), dma,
        ],
        compiler_params=pltpu.CompilerParams(
            collective_id=0, has_side_effects=True, vmem_limit_bytes=58 << 20
        ),
    )(
        tile_mask.reshape(2, 2),
        queries.reshape(frame),
        keys_spatial.reshape(frame),
        values_spatial.reshape(frame),
        temporal_keys.reshape(blocks),
        temporal_values.reshape(blocks),
        query_weight,
        out_grad.reshape(blocks),
    )
    whole = (1, 1, PATCH, WIDTH)
    return (*(a.reshape(whole) for a in (d_q, d_k, d_v, d_tk, d_tv)), d_w)


def solution(mesh):
    framed = P("dp", "seq", None, None)
    return jax.shard_map(
        per_device,
        mesh=mesh,
        in_specs=(framed,) * 6 + (P("seq", None), P("dp", None, "seq", None)),
        out_specs=(framed,) * 5 + (P("seq", None),),
        check_vma=False,
    )
```

```python
import math

import jax
import jax.numpy as jnp
from jax import lax
from jax.experimental import pallas as pl
from jax.experimental.pallas import tpu as pltpu
from jax.sharding import PartitionSpec as P

HEADS = 12
HEAD_DIM = 128
TILE = 128
WIDTH = HEADS * HEAD_DIM
NX, NY, NZ = 4, 4, 8
SEQ = NZ * NY
ROWS = 48
PATCH = 256
PAIR = 2 * HEAD_DIM
PAIRS = WIDTH // PAIR
CHUNK = 512
THIRDS = WIDTH // CHUNK
COLS = WIDTH // NX
SCALE = 1.0 / math.sqrt(HEAD_DIM)
SCALE2 = SCALE * math.log2(math.e)
EPS = 1e-06
MESH = pl.DeviceIdType.MESH
F32 = jnp.float32
BF16 = jnp.bfloat16


def dot(a, b, contract):
    return lax.dot_general(a, b, ((contract[:1], contract[1:]), ((), ())), preferred_element_type=F32)


def inverse_rms(a):
    return lax.rsqrt(jnp.mean(a * a, axis=-1, keepdims=True) + EPS)


def norm_back(grad, normed, inverse):
    return (inverse * SCALE) * (grad - normed * jnp.mean(grad * normed, axis=-1, keepdims=True))


def softmax(q_norm, k_norm, mask):
    exps = jnp.exp2(dot(q_norm, k_norm, (1, 1)) * SCALE2) * mask
    return exps * (1.0 / jnp.sum(exps, axis=-1, keepdims=True))


def attention_back(weights, weights_b, q, k, qn, kn, rq, rk, qn_b, kn_b, v, grad):
    d_weights = dot(grad, v, (1, 1))
    delta = jnp.sum(weights * d_weights, axis=-1, keepdims=True)
    d_scores = (weights * (d_weights - delta)).astype(BF16)
    d_v = dot(weights_b, grad, (0, 0))
    d_q = norm_back(dot(d_scores, kn_b, (1, 0)), qn, rq)
    d_k = norm_back(dot(d_scores, qn_b, (0, 0)), kn, rk)
    return d_q, d_k, d_v


def wait_for(ref, sem):
    pltpu.make_async_copy(ref, ref, sem).wait()


def kernel(
    tile_ref, q_in, k_in, v_in, tk_ref, tv_ref, w_in_ref, og_in,
    dq_ref, dk_ref, dv_ref, dtk_ref, dtv_ref, dw_ref,
    q_ref, k_ref, v_ref, og_ref, w_ref, weight, mask, tmask, spatial, k_buf, v_buf, s_buf, s_mat, d_mat, attn,
    dk_send, dv_send, ds_send, ds_buf,
    part, core_in, x_in, x_sum, y_in, y_sum, z_in, final,
    load, send, a2a_in, tk_in, tv_in, tk_out, tv_out, s_out, dk_out, dv_out, wz_in, wy_in, wx_in, wc_in,
    core_sem, x_sem, y_sem, z_sem, out_sem, g_send,
):
    d = lax.axis_index("dp")
    s = lax.axis_index("seq")
    x, c = d // 2, d % 2
    z, y = s // NY, s % NY
    sibling = {"dp": x * 2 + 1 - c}
    active = y % 2 == c
    idle = y % 2 != c

    def seq_peer(o):
        return lax.rem(s + o, SEQ)

    def x_peer(o):
        return {"dp": lax.rem(x + o, NX) * 2 + c}

    def y_peer(o):
        return {"seq": z * NY + lax.rem(y + o, NY)}

    def z_peer(o):
        return {"seq": lax.rem(z + o, NZ) * NY + y}

    def remote(src, dst, send_sem, recv_sem, device):
        pltpu.make_async_remote_copy(
            src, dst, send_sem, recv_sem, device_id=device, device_id_type=MESH
        ).start()

    def exchange(src, dst, lanes, send_sem, recv_sem):
        pltpu.make_async_copy(src.at[s, :, lanes], dst.at[s, :, lanes], recv_sem).start()

        @pl.loop(1, SEQ)
        def _(o):
            j = seq_peer(o)
            remote(src.at[j, :, lanes], dst.at[s, :, lanes], send_sem, recv_sem, {"seq": j})

    def lanes_of(n, width):
        return pl.ds(pl.multiple_of(n * width, width), width)

    own_cols = lanes_of(x, COLS)

    def chunk_of(g):
        return lanes_of(g, CHUNK)

    loads = ((w_in_ref, w_ref), (q_in, q_ref), (k_in, k_ref), (v_in, v_ref), (og_in, og_ref))
    for i, (src, dst) in enumerate(loads):
        pltpu.make_async_copy(src, dst, load.at[i]).start()

    wait_for(w_ref, load.at[0])
    weight[z, y] = w_ref[...]

    barrier = pltpu.get_barrier_semaphore()

    @pl.loop(1, SEQ)
    def _(o):
        pl.semaphore_signal(barrier, inc=1, device_id={"seq": seq_peer(o)}, device_id_type=MESH)

    @pl.loop(1, 2 * NX)
    def _(o):
        pl.semaphore_signal(barrier, inc=1, device_id={"dp": lax.rem(d + o, 2 * NX)}, device_id_type=MESH)

    ones = jnp.ones((TILE, TILE), F32)
    for a in range(2):
        for b in range(2):
            value = 1.0 if a == b else jnp.where(tile_ref[a, b] == 1, 1.0, 0.0).astype(F32)
            mask[a * TILE:(a + 1) * TILE, b * TILE:(b + 1) * TILE] = ones * value
    row = lax.broadcasted_iota(jnp.int32, (PATCH, PATCH), 0)
    col = lax.broadcasted_iota(jnp.int32, (PATCH, PATCH), 1)
    tmask[...] = jnp.where(row % 8 == col % 8, 1.0, 0.0).astype(F32)

    pl.semaphore_wait(barrier, SEQ - 1 + 2 * NX - 1)

    def cols_of(xs, g):
        return pl.ds(pl.multiple_of(xs * COLS + g * HEAD_DIM, HEAD_DIM), HEAD_DIM)

    for g in range(THIRDS):
        @pl.when(active)
        def _():
            src = weight.at[z, y, :, cols_of(x, g)]

            @pl.loop(1, NZ)
            def _(o):
                remote(src, src, send.at[0], wz_in.at[g], z_peer(o))

    exchange(tk_ref, k_buf, chunk_of(0), tk_out.at[0], tk_in.at[0])

    for i in (1, 2, 3):
        wait_for(loads[i][1], load.at[i])

    @pl.loop(0, PAIRS)
    def _(n):
        lanes = lanes_of(n, PAIR)
        q2, k2 = q_ref[:, lanes].astype(F32), k_ref[:, lanes].astype(F32)
        v2 = v_ref[:, lanes]
        outs = []
        for h in range(2):
            cut = slice(h * HEAD_DIM, (h + 1) * HEAD_DIM)
            q, k = q2[:, cut], k2[:, cut]
            qn = (q * inverse_rms(q)).astype(BF16)
            kn = (k * inverse_rms(k)).astype(BF16)
            weights = softmax(qn, kn, mask[...]).astype(BF16)
            attn[2 * n + h] = weights
            outs.append(dot(weights, v2[:, cut], (1, 0)))
        out = jnp.concatenate(outs, axis=1)
        spatial[:, :, lanes] = out.reshape(SEQ, 8, PAIR).astype(BF16)

        @pl.when(n % 2 == 1)
        def _():
            exchange(spatial, s_buf, chunk_of(n // 2), s_out.at[n // 2], a2a_in.at[1])

    def sent(sem):
        wait_for(k_buf.at[pl.ds(0, SEQ - 1), :, pl.ds(0, CHUNK)], sem)

    def send_k(g):
        exchange(tk_ref, k_buf, chunk_of(g), tk_out.at[g], tk_in.at[g])

    def send_v(g):
        exchange(tv_ref, v_buf, chunk_of(g), tv_out.at[g], tv_in.at[g])

    for g in range(THIRDS):
        @pl.when(active)
        def _():
            wait_for(weight.at[pl.ds(0, NZ - 1), y, :, cols_of(x, g)], wz_in.at[g])
            src = weight.at[:, y, :, cols_of(x, g)]

            @pl.loop(1, NY)
            def _(o):
                remote(src, src, send.at[1], wy_in.at[g], y_peer(o))

    sent(tk_out.at[0])
    send_v(0)

    for g in range(THIRDS):
        @pl.when(active)
        def _():
            wait_for(weight.at[:, 0, :, cols_of(x, g)], wy_in.at[g])

        @pl.when(idle)
        def _():
            wait_for(weight.at[:, pl.ds(0, 2), :, cols_of(x, g)], wy_in.at[g])

        for h in range(2):
            src = weight.at[:, c + 2 * h, :, cols_of(x, g)]

            @pl.loop(1, NX)
            def _(o):
                remote(src, src, send.at[2], wx_in.at[g, o - 1], x_peer(o))

            remote(src, src, send.at[3], wc_in, sibling)

    sent(s_out.at[0])
    send_k(1)
    sent(s_out.at[1])
    send_v(1)

    for g in range(THIRDS):
        for o in (1, 3, 2):
            cols = cols_of(lax.rem(x + NX - o, NX), g)
            wait_for(weight.at[:, pl.ds(0, 2), :, cols], wx_in.at[g, o - 1])
            for h in range(2):
                src = weight.at[:, c + 2 * h, :, cols]
                remote(src, src, send.at[3], wc_in, sibling)
        if g == 0:
            sent(s_out.at[2])
            send_k(2)
        if g == 1:
            sent(tv_out.at[0])
            send_v(2)

    wait_for(s_buf, a2a_in.at[1])
    for n in range(PAIRS):
        lanes = slice(n * PAIR, (n + 1) * PAIR)
        s_mat[:, lanes] = s_buf[:, :, lanes].astype(F32).reshape(PATCH, PAIR).astype(BF16)
    wait_for(weight.at[:, pl.ds(0, 2)], wc_in)
    wait_for(og_ref, load.at[4])

    def part_step(g):
        cols = d_mat[:, chunk_of(g)]

        @pl.loop(0, NZ // 2)
        def _(m):
            block = dot(s_mat[:, lanes_of(m, 2 * NY * ROWS)], cols, (0, 0))
            part[g, pl.ds(2 * m, 2)] = block.reshape(2, NY, ROWS, CHUNK).astype(BF16)

        for h in range(2):
            remote(part.at[g, :, 1 - c + 2 * h], core_in.at[g, h], g_send.at[0], core_sem.at[g], sibling)

    def x_step(g):
        wait_for(core_in.at[g], core_sem.at[g])
        for h in range(2):
            own = part[g, :, c + 2 * h].astype(F32) + core_in[g, h].astype(F32)
            part[g, :, c + 2 * h] = own.astype(BF16)

            @pl.loop(1, NX)
            def _(o):
                to = lax.rem(x + o, NX)
                remote(
                    part.at[g, :, c + 2 * h, :, lanes_of(to, HEAD_DIM)], x_in.at[g, o - 1, h],
                    g_send.at[1], x_sem.at[g], x_peer(o),
                )

    def y_step(g):
        wait_for(x_in.at[g], x_sem.at[g])
        for h in range(2):
            total = part[g, :, c + 2 * h, :, lanes_of(x, HEAD_DIM)].astype(F32)
            for o in range(NX - 1):
                total = total + x_in[g, o, h].astype(F32)
            x_sum[g, h] = total.astype(BF16)
            owner = c + 2 * h

            @pl.when(y != owner)
            def _():
                away = lax.rem(y - owner + NY, NY)
                remote(x_sum.at[g, h], y_in.at[g, away - 1], g_send.at[2], y_sem.at[g], {"seq": z * NY + owner})

    def z_step(g):
        @pl.when(active)
        def _():
            wait_for(y_in.at[g], y_sem.at[g])
            total = x_sum[g, y // 2].astype(F32)
            for o in range(NY - 1):
                total = total + y_in[g, o].astype(F32)
            y_sum[g] = total.astype(BF16)

            @pl.loop(1, NZ)
            def _(o):
                remote(
                    y_sum.at[g, lax.rem(z + o, NZ)], z_in.at[g, o - 1], g_send.at[3], z_sem.at[g], z_peer(o)
                )

    def out_step(g):
        @pl.when(active)
        def _():
            wait_for(z_in.at[g], z_sem.at[g])
            total = y_sum[g, z].astype(F32)
            for o in range(NZ - 1):
                total = total + z_in[g, o].astype(F32)
            final[g] = total.astype(BF16)
            dst = dw_ref.at[:, pl.ds(pl.multiple_of(g * CHUNK + x * HEAD_DIM, HEAD_DIM), HEAD_DIM)]
            pltpu.make_async_copy(final.at[g], dst, out_sem).start()

            @pl.loop(1, 2 * NX)
            def _(o):
                remote(final.at[g], dst, g_send.at[4], out_sem, {"dp": lax.rem(d + o, 2 * NX)})

    @pl.loop(0, PAIRS)
    def _(n):
        lanes = lanes_of(n, PAIR)

        @pl.when(n % 2 == 0)
        def _():
            g = n // 2
            wait_for(k_buf.at[:, :, chunk_of(g)], tk_in.at[g])
            wait_for(v_buf.at[:, :, chunk_of(g)], tv_in.at[g])

        rows = weight[:, :, :, lanes].reshape(WIDTH, PAIR)
        q2 = dot(s_mat[...], rows, (1, 0)).astype(BF16).astype(F32)
        k2 = k_buf[:, :, lanes].astype(F32).reshape(PATCH, PAIR)
        v2 = v_buf[:, :, lanes].astype(F32).reshape(PATCH, PAIR).astype(BF16)
        g2 = og_ref[:, :, lanes].astype(F32).reshape(PATCH, PAIR).astype(BF16)
        d_qs, d_ks, d_vs = [], [], []
        for h in range(2):
            cut = slice(h * HEAD_DIM, (h + 1) * HEAD_DIM)
            q, k = q2[:, cut], k2[:, cut]
            rq, rk = inverse_rms(q), inverse_rms(k)
            qn, kn = q * rq, k * rk
            qn_b, kn_b = qn.astype(BF16), kn.astype(BF16)
            weights = softmax(qn_b, kn_b, tmask[...])
            d_q, d_k, d_v = attention_back(
                weights, weights.astype(BF16), q, k, qn, kn, rq, rk, qn_b, kn_b, v2[:, cut], g2[:, cut]
            )
            d_qs.append(d_q)
            d_ks.append(d_k)
            d_vs.append(d_v)
        d_mat[:, lanes] = jnp.concatenate(d_qs, axis=1).astype(BF16)
        dk_send[:, :, lanes] = jnp.concatenate(d_ks, axis=1).reshape(SEQ, 8, PAIR).astype(BF16)
        dv_send[:, :, lanes] = jnp.concatenate(d_vs, axis=1).reshape(SEQ, 8, PAIR).astype(BF16)

        @pl.when(n % 2 == 1)
        def _():
            part_step(n // 2)

        @pl.when(n == 3)
        def _():
            x_step(0)

        @pl.when(n == 5)
        def _():
            x_step(1)

        @pl.when(n == 1)
        def _():
            first = pl.ds(0, CHUNK)
            exchange(dk_send, dtk_ref, first, dk_out.at[0], a2a_in.at[3])
            exchange(dv_send, dtv_ref, first, dv_out.at[0], a2a_in.at[4])

    @pl.loop(0, NZ // 2)
    def _(m):
        rows = weight[pl.ds(2 * m, 2)].reshape(2 * NY * ROWS, WIDTH)
        out = dot(d_mat[...], rows, (1, 1))
        lanes = lanes_of(m, 2 * NY * ROWS)
        ds_send[:, :, lanes] = out.reshape(SEQ, 8, 2 * NY * ROWS).astype(BF16)
        exchange(ds_send, ds_buf, lanes, send.at[4], a2a_in.at[5])

    def send_back(g):
        exchange(dk_send, dtk_ref, chunk_of(g), dk_out.at[g], a2a_in.at[3])
        exchange(dv_send, dtv_ref, chunk_of(g), dv_out.at[g], a2a_in.at[4])

    x_step(2)
    sent(dk_out.at[0])
    sent(dv_out.at[0])
    send_back(1)
    y_step(0)
    y_step(1)
    z_step(0)
    send_back(2)
    y_step(2)
    z_step(1)

    wait_for(ds_buf, a2a_in.at[5])

    @pl.loop(0, PAIRS)
    def _(n):
        lanes = lanes_of(n, PAIR)
        q2, k2 = q_ref[:, lanes].astype(F32), k_ref[:, lanes].astype(F32)
        v2 = v_ref[:, lanes]
        g2 = ds_buf[:, :, lanes].astype(F32).reshape(PATCH, PAIR).astype(BF16)
        d_qs, d_ks, d_vs = [], [], []
        for h in range(2):
            cut = slice(h * HEAD_DIM, (h + 1) * HEAD_DIM)
            q, k = q2[:, cut], k2[:, cut]
            rq, rk = inverse_rms(q), inverse_rms(k)
            qn, kn = q * rq, k * rk
            weights = attn[2 * n + h]
            d_q, d_k, d_v = attention_back(
                weights.astype(F32), weights, q, k, qn, kn, rq, rk, qn.astype(BF16), kn.astype(BF16),
                v2[:, cut], g2[:, cut],
            )
            d_qs.append(d_q)
            d_ks.append(d_k)
            d_vs.append(d_v)
        dq_ref[:, lanes] = jnp.concatenate(d_qs, axis=1).astype(BF16)
        dk_ref[:, lanes] = jnp.concatenate(d_ks, axis=1).astype(BF16)
        dv_ref[:, lanes] = jnp.concatenate(d_vs, axis=1).astype(BF16)

        @pl.when(n == 1)
        def _():
            z_step(2)
            out_step(0)

        @pl.when(n == 3)
        def _():
            out_step(1)

    out_step(2)

    wait_for(dtk_ref, a2a_in.at[3])
    wait_for(dtv_ref, a2a_in.at[4])

    wait_for(dw_ref, out_sem)

    for sem in (tk_out.at[1], tk_out.at[2], tv_out.at[1], tv_out.at[2]):
        sent(sem)
    for sem in (dk_out.at[1], dk_out.at[2], dv_out.at[1], dv_out.at[2]):
        sent(sem)
    wait_for(ds_buf.at[pl.ds(0, SEQ - 1)], send.at[4])
    wait_for(weight.at[:, pl.ds(0, 2), :, pl.ds(0, 3 * COLS)], send.at[2])
    wait_for(weight.at[:, pl.ds(0, 2)], send.at[3])
    wait_for(core_in, g_send.at[0])
    wait_for(x_in, g_send.at[1])

    @pl.when(active)
    def _():
        wait_for(weight.at[pl.ds(0, NZ - 1), y, :, own_cols], send.at[0])
        wait_for(weight.at[:, 0, :, pl.ds(0, 3 * COLS)], send.at[1])
        wait_for(x_sum.at[:, 0], g_send.at[2])
        wait_for(z_in, g_send.at[3])
        wait_for(z_in, g_send.at[4])

    @pl.when(idle)
    def _():
        wait_for(x_sum, g_send.at[2])


def store(*refs):
    copies = [pltpu.make_async_copy(refs[i], refs[6 + i], refs[12].at[i]) for i in range(6)]
    for copy in copies:
        copy.start()
    for copy in copies:
        copy.wait()


def per_device(
    queries, keys_spatial, values_spatial, temporal_keys, temporal_values, tile_mask, query_weight, out_grad
):
    frame = (PATCH, WIDTH)
    blocks = (SEQ, 8, WIDTH)
    vmem = pl.BlockSpec(memory_space=pltpu.VMEM)
    smem = pl.BlockSpec(memory_space=pltpu.SMEM)
    anywhere = pl.BlockSpec(memory_space=pl.ANY)
    dma = pltpu.SemaphoreType.DMA

    def buf(*shape, kind=BF16):
        return pltpu.VMEM(shape, kind)

    results = pl.pallas_call(
        kernel,
        out_shape=(
            *(pltpu.VMEM(frame, BF16) for _ in range(3)),
            *(pltpu.VMEM(blocks, BF16) for _ in range(2)),
            pltpu.VMEM((ROWS, WIDTH), BF16),
        ),
        in_specs=[smem] + [anywhere] * 7,
        out_specs=(vmem,) * 6,
        scratch_shapes=[
            buf(*frame), buf(*frame), buf(*frame), buf(*blocks), buf(ROWS, WIDTH),
            buf(NZ, NY, ROWS, WIDTH),
            buf(PATCH, PATCH, kind=F32),
            buf(PATCH, PATCH, kind=F32),
            buf(*blocks), buf(*blocks), buf(*blocks), buf(*blocks),
            buf(*frame), buf(*frame),
            buf(HEADS, PATCH, PATCH),
            buf(*blocks), buf(*blocks), buf(*blocks), buf(*blocks),
            buf(THIRDS, NZ, NY, ROWS, CHUNK),
            buf(THIRDS, 2, NZ, ROWS, CHUNK),
            buf(THIRDS, NX - 1, 2, NZ, ROWS, HEAD_DIM),
            buf(THIRDS, 2, NZ, ROWS, HEAD_DIM),
            buf(THIRDS, NY - 1, NZ, ROWS, HEAD_DIM),
            buf(THIRDS, NZ, ROWS, HEAD_DIM),
            buf(THIRDS, NZ - 1, ROWS, HEAD_DIM),
            buf(THIRDS, ROWS, HEAD_DIM),
            dma((5,)), dma((5,)), dma((6,)), *(dma((THIRDS,)) for _ in range(9)), dma((THIRDS, NX - 1)), dma,
            dma((THIRDS,)), dma((THIRDS,)), dma((THIRDS,)), dma((THIRDS,)), dma, dma((5,)),
        ],
        compiler_params=pltpu.CompilerParams(
            collective_id=0, has_side_effects=True, vmem_limit_bytes=56 << 20
        ),
    )(
        tile_mask.reshape(2, 2),
        queries.reshape(frame),
        keys_spatial.reshape(frame),
        values_spatial.reshape(frame),
        temporal_keys.reshape(blocks),
        temporal_values.reshape(blocks),
        query_weight,
        out_grad.reshape(blocks),
    )
    d_q, d_k, d_v, d_tk, d_tv, d_w = pl.pallas_call(
        store,
        out_shape=tuple(jax.ShapeDtypeStruct(a.shape, a.dtype) for a in results),
        in_specs=[anywhere] * 6,
        out_specs=(anywhere,) * 6,
        scratch_shapes=[dma((6,))],
        compiler_params=pltpu.CompilerParams(vmem_limit_bytes=1 << 20),
    )(*results)
    whole = (1, 1, PATCH, WIDTH)
    return (*(a.reshape(whole) for a in (d_q, d_k, d_v, d_tk, d_tv)), d_w)


def solution(mesh):
    framed = P("dp", "seq", None, None)
    return jax.shard_map(
        per_device,
        mesh=mesh,
        in_specs=(framed,) * 6 + (P("seq", None), P("dp", None, "seq", None)),
        out_specs=(framed,) * 5 + (P("seq", None),),
        check_vma=False,
    )
```

```python
import math

import jax
import jax.numpy as jnp
from jax import lax
from jax.experimental import pallas as pl
from jax.experimental.pallas import tpu as pltpu
from jax.sharding import PartitionSpec as P

HEADS = 12
HEAD_DIM = 128
TILE = 128
WIDTH = HEADS * HEAD_DIM
NX, NY, NZ = 4, 4, 8
SEQ = NZ * NY
ROWS = 48
PATCH = 256
PAIR = 2 * HEAD_DIM
PAIRS = WIDTH // PAIR
CHUNK = 512
THIRDS = WIDTH // CHUNK
COLS = WIDTH // NX
SCALE = 1.0 / math.sqrt(HEAD_DIM)
SCALE2 = SCALE * math.log2(math.e)
EPS = 1e-06
MESH = pl.DeviceIdType.MESH
F32 = jnp.float32
BF16 = jnp.bfloat16


def dot(a, b, contract):
    return lax.dot_general(a, b, ((contract[:1], contract[1:]), ((), ())), preferred_element_type=F32)


def inverse_rms(a):
    return lax.rsqrt(jnp.mean(a * a, axis=-1, keepdims=True) + EPS)


def norm_back(grad, normed, inverse):
    return (inverse * SCALE) * (grad - normed * jnp.mean(grad * normed, axis=-1, keepdims=True))


def softmax(q_norm, k_norm, mask):
    exps = jnp.exp2(dot(q_norm, k_norm, (1, 1)) * SCALE2) * mask
    return exps * (1.0 / jnp.sum(exps, axis=-1, keepdims=True))


def attention_back(weights, weights_b, q, k, qn, kn, rq, rk, qn_b, kn_b, v, grad):
    d_weights = dot(grad, v, (1, 1))
    delta = jnp.sum(weights * d_weights, axis=-1, keepdims=True)
    d_scores = (weights * (d_weights - delta)).astype(BF16)
    d_v = dot(weights_b, grad, (0, 0))
    d_q = norm_back(dot(d_scores, kn_b, (1, 0)), qn, rq)
    d_k = norm_back(dot(d_scores, qn_b, (0, 0)), kn, rk)
    return d_q, d_k, d_v


def wait_for(ref, sem):
    pltpu.make_async_copy(ref, ref, sem).wait()


def kernel(
    tile_ref, q_in, k_in, v_in, tk_ref, tv_ref, w_in_ref, og_in,
    dq_ref, dk_ref, dv_ref, dtk_ref, dtv_ref, dw_ref,
    q_ref, k_ref, v_ref, og_ref, w_ref, weight, mask, tmask, spatial, k_buf, v_buf, s_buf, s_mat, d_mat, attn,
    dk_send, dv_send, ds_send, ds_buf,
    part, core_in, x_in, x_sum, y_in, y_sum, z_in, final,
    load, send, a2a_in, tk_in, tv_in, tk_out, tv_out, s_out, dk_out, dv_out, wz_in, wy_in, wx_in, wc_in,
    core_sem, x_sem, y_sem, z_sem, out_sem, g_send,
):
    d = lax.axis_index("dp")
    s = lax.axis_index("seq")
    x, c = d // 2, d % 2
    z, y = s // NY, s % NY
    sibling = {"dp": x * 2 + 1 - c}
    active = y % 2 == c
    idle = y % 2 != c

    def seq_peer(o):
        return lax.rem(s + o, SEQ)

    def x_peer(o):
        return {"dp": lax.rem(x + o, NX) * 2 + c}

    def y_peer(o):
        return {"seq": z * NY + lax.rem(y + o, NY)}

    def z_peer(o):
        return {"seq": lax.rem(z + o, NZ) * NY + y}

    def remote(src, dst, send_sem, recv_sem, device):
        pltpu.make_async_remote_copy(
            src, dst, send_sem, recv_sem, device_id=device, device_id_type=MESH
        ).start()

    def exchange(src, dst, lanes, send_sem, recv_sem):
        pltpu.make_async_copy(src.at[s, :, lanes], dst.at[s, :, lanes], recv_sem).start()

        @pl.loop(1, SEQ)
        def _(o):
            j = seq_peer(o)
            remote(src.at[j, :, lanes], dst.at[s, :, lanes], send_sem, recv_sem, {"seq": j})

    def lanes_of(n, width):
        return pl.ds(pl.multiple_of(n * width, width), width)

    own_cols = lanes_of(x, COLS)

    def chunk_of(g):
        return lanes_of(g, CHUNK)

    loads = ((w_in_ref, w_ref), (q_in, q_ref), (k_in, k_ref), (v_in, v_ref), (og_in, og_ref))
    for i, (src, dst) in enumerate(loads):
        pltpu.make_async_copy(src, dst, load.at[i]).start()

    wait_for(w_ref, load.at[0])
    weight[z, y] = w_ref[...]

    barrier = pltpu.get_barrier_semaphore()

    @pl.loop(1, SEQ)
    def _(o):
        pl.semaphore_signal(barrier, inc=1, device_id={"seq": seq_peer(o)}, device_id_type=MESH)

    @pl.loop(1, 2 * NX)
    def _(o):
        pl.semaphore_signal(barrier, inc=1, device_id={"dp": lax.rem(d + o, 2 * NX)}, device_id_type=MESH)

    ones = jnp.ones((TILE, TILE), F32)
    for a in range(2):
        for b in range(2):
            value = 1.0 if a == b else jnp.where(tile_ref[a, b] == 1, 1.0, 0.0).astype(F32)
            mask[a * TILE:(a + 1) * TILE, b * TILE:(b + 1) * TILE] = ones * value
    row = lax.broadcasted_iota(jnp.int32, (PATCH, PATCH), 0)
    col = lax.broadcasted_iota(jnp.int32, (PATCH, PATCH), 1)
    tmask[...] = jnp.where(row % 8 == col % 8, 1.0, 0.0).astype(F32)

    pl.semaphore_wait(barrier, SEQ - 1 + 2 * NX - 1)

    def cols_of(xs, g):
        return pl.ds(pl.multiple_of(xs * COLS + g * HEAD_DIM, HEAD_DIM), HEAD_DIM)

    for g in range(THIRDS):
        @pl.when(active)
        def _():
            src = weight.at[z, y, :, cols_of(x, g)]

            @pl.loop(1, NZ)
            def _(o):
                remote(src, src, send.at[0], wz_in.at[g], z_peer(o))

    exchange(tk_ref, k_buf, chunk_of(0), tk_out.at[0], tk_in.at[0])

    for i in (1, 2, 3):
        wait_for(loads[i][1], load.at[i])

    @pl.loop(0, PAIRS)
    def _(n):
        lanes = lanes_of(n, PAIR)
        q2, k2 = q_ref[:, lanes].astype(F32), k_ref[:, lanes].astype(F32)
        v2 = v_ref[:, lanes]
        outs = []
        for h in range(2):
            cut = slice(h * HEAD_DIM, (h + 1) * HEAD_DIM)
            q, k = q2[:, cut], k2[:, cut]
            qn = (q * inverse_rms(q)).astype(BF16)
            kn = (k * inverse_rms(k)).astype(BF16)
            weights = softmax(qn, kn, mask[...]).astype(BF16)
            attn[2 * n + h] = weights
            outs.append(dot(weights, v2[:, cut], (1, 0)))
        out = jnp.concatenate(outs, axis=1)
        spatial[:, :, lanes] = out.reshape(SEQ, 8, PAIR).astype(BF16)

        @pl.when(n % 2 == 1)
        def _():
            exchange(spatial, s_buf, chunk_of(n // 2), s_out.at[n // 2], a2a_in.at[1])

    def sent(sem):
        wait_for(k_buf.at[pl.ds(0, SEQ - 1), :, pl.ds(0, CHUNK)], sem)

    def send_k(g):
        exchange(tk_ref, k_buf, chunk_of(g), tk_out.at[g], tk_in.at[g])

    def send_v(g):
        exchange(tv_ref, v_buf, chunk_of(g), tv_out.at[g], tv_in.at[g])

    for g in range(THIRDS):
        @pl.when(active)
        def _():
            wait_for(weight.at[pl.ds(0, NZ - 1), y, :, cols_of(x, g)], wz_in.at[g])
            src = weight.at[:, y, :, cols_of(x, g)]

            @pl.loop(1, NY)
            def _(o):
                remote(src, src, send.at[1], wy_in.at[g], y_peer(o))

    sent(tk_out.at[0])
    send_v(0)

    for g in range(THIRDS):
        @pl.when(active)
        def _():
            wait_for(weight.at[:, 0, :, cols_of(x, g)], wy_in.at[g])

        @pl.when(idle)
        def _():
            wait_for(weight.at[:, pl.ds(0, 2), :, cols_of(x, g)], wy_in.at[g])

        for h in range(2):
            src = weight.at[:, c + 2 * h, :, cols_of(x, g)]

            @pl.loop(1, NX)
            def _(o):
                remote(src, src, send.at[2], wx_in.at[g, o - 1], x_peer(o))

            remote(src, src, send.at[3], wc_in, sibling)

    sent(s_out.at[0])
    send_k(1)
    sent(s_out.at[1])
    send_v(1)

    for g in range(THIRDS):
        for o in (1, 3, 2):
            cols = cols_of(lax.rem(x + NX - o, NX), g)
            wait_for(weight.at[:, pl.ds(0, 2), :, cols], wx_in.at[g, o - 1])
            for h in range(2):
                src = weight.at[:, c + 2 * h, :, cols]
                remote(src, src, send.at[3], wc_in, sibling)
        if g == 0:
            sent(s_out.at[2])
            send_k(2)
        if g == 1:
            sent(tv_out.at[0])
            send_v(2)

    wait_for(s_buf, a2a_in.at[1])
    for n in range(PAIRS):
        lanes = slice(n * PAIR, (n + 1) * PAIR)
        s_mat[:, lanes] = s_buf[:, :, lanes].astype(F32).reshape(PATCH, PAIR).astype(BF16)
    wait_for(weight.at[:, pl.ds(0, 2)], wc_in)
    wait_for(og_ref, load.at[4])

    def part_step(g):
        cols = d_mat[:, chunk_of(g)]

        @pl.loop(0, NZ // 2)
        def _(m):
            block = dot(s_mat[:, lanes_of(m, 2 * NY * ROWS)], cols, (0, 0))
            part[g, pl.ds(2 * m, 2)] = block.reshape(2, NY, ROWS, CHUNK).astype(BF16)

        for h in range(2):
            remote(part.at[g, :, 1 - c + 2 * h], core_in.at[g, h], g_send.at[0], core_sem.at[g], sibling)

    def x_step(g):
        wait_for(core_in.at[g], core_sem.at[g])
        for h in range(2):
            own = part[g, :, c + 2 * h].astype(F32) + core_in[g, h].astype(F32)
            part[g, :, c + 2 * h] = own.astype(BF16)

            @pl.loop(1, NX)
            def _(o):
                to = lax.rem(x + o, NX)
                remote(
                    part.at[g, :, c + 2 * h, :, lanes_of(to, HEAD_DIM)], x_in.at[g, o - 1, h],
                    g_send.at[1], x_sem.at[g], x_peer(o),
                )

    def y_step(g):
        wait_for(x_in.at[g], x_sem.at[g])
        for h in range(2):
            total = part[g, :, c + 2 * h, :, lanes_of(x, HEAD_DIM)].astype(F32)
            for o in range(NX - 1):
                total = total + x_in[g, o, h].astype(F32)
            x_sum[g, h] = total.astype(BF16)
            owner = c + 2 * h

            @pl.when(y != owner)
            def _():
                away = lax.rem(y - owner + NY, NY)
                remote(x_sum.at[g, h], y_in.at[g, away - 1], g_send.at[2], y_sem.at[g], {"seq": z * NY + owner})

    def z_step(g):
        @pl.when(active)
        def _():
            wait_for(y_in.at[g], y_sem.at[g])
            total = x_sum[g, y // 2].astype(F32)
            for o in range(NY - 1):
                total = total + y_in[g, o].astype(F32)
            y_sum[g] = total.astype(BF16)

            @pl.loop(1, NZ)
            def _(o):
                remote(
                    y_sum.at[g, lax.rem(z + o, NZ)], z_in.at[g, o - 1], g_send.at[3], z_sem.at[g], z_peer(o)
                )

    def out_step(g):
        @pl.when(active)
        def _():
            wait_for(z_in.at[g], z_sem.at[g])
            total = y_sum[g, z].astype(F32)
            for o in range(NZ - 1):
                total = total + z_in[g, o].astype(F32)
            final[g] = total.astype(BF16)
            dst = dw_ref.at[:, pl.ds(pl.multiple_of(g * CHUNK + x * HEAD_DIM, HEAD_DIM), HEAD_DIM)]
            pltpu.make_async_copy(final.at[g], dst, out_sem).start()

            @pl.loop(1, 2 * NX)
            def _(o):
                remote(final.at[g], dst, g_send.at[4], out_sem, {"dp": lax.rem(d + o, 2 * NX)})

    @pl.loop(0, PAIRS)
    def _(n):
        lanes = lanes_of(n, PAIR)

        @pl.when(n % 2 == 0)
        def _():
            g = n // 2
            wait_for(k_buf.at[:, :, chunk_of(g)], tk_in.at[g])
            wait_for(v_buf.at[:, :, chunk_of(g)], tv_in.at[g])

        rows = weight[:, :, :, lanes].reshape(WIDTH, PAIR)
        q2 = dot(s_mat[...], rows, (1, 0)).astype(BF16).astype(F32)
        k2 = k_buf[:, :, lanes].astype(F32).reshape(PATCH, PAIR)
        v2 = v_buf[:, :, lanes].astype(F32).reshape(PATCH, PAIR).astype(BF16)
        g2 = og_ref[:, :, lanes].astype(F32).reshape(PATCH, PAIR).astype(BF16)
        d_qs, d_ks, d_vs = [], [], []
        for h in range(2):
            cut = slice(h * HEAD_DIM, (h + 1) * HEAD_DIM)
            q, k = q2[:, cut], k2[:, cut]
            rq, rk = inverse_rms(q), inverse_rms(k)
            qn, kn = q * rq, k * rk
            qn_b, kn_b = qn.astype(BF16), kn.astype(BF16)
            weights = softmax(qn_b, kn_b, tmask[...])
            d_q, d_k, d_v = attention_back(
                weights, weights.astype(BF16), q, k, qn, kn, rq, rk, qn_b, kn_b, v2[:, cut], g2[:, cut]
            )
            d_qs.append(d_q)
            d_ks.append(d_k)
            d_vs.append(d_v)
        d_mat[:, lanes] = jnp.concatenate(d_qs, axis=1).astype(BF16)
        dk_send[:, :, lanes] = jnp.concatenate(d_ks, axis=1).reshape(SEQ, 8, PAIR).astype(BF16)
        dv_send[:, :, lanes] = jnp.concatenate(d_vs, axis=1).reshape(SEQ, 8, PAIR).astype(BF16)

        @pl.when(n % 2 == 1)
        def _():
            part_step(n // 2)

        @pl.when(n == 3)
        def _():
            x_step(0)

        @pl.when(n == 5)
        def _():
            x_step(1)

        @pl.when(n == 1)
        def _():
            first = pl.ds(0, CHUNK)
            exchange(dk_send, dtk_ref, first, dk_out.at[0], a2a_in.at[3])
            exchange(dv_send, dtv_ref, first, dv_out.at[0], a2a_in.at[4])

    @pl.loop(0, NZ // 2)
    def _(m):
        rows = weight[pl.ds(2 * m, 2)].reshape(2 * NY * ROWS, WIDTH)
        out = dot(d_mat[...], rows, (1, 1))
        lanes = lanes_of(m, 2 * NY * ROWS)
        ds_send[:, :, lanes] = out.reshape(SEQ, 8, 2 * NY * ROWS).astype(BF16)
        exchange(ds_send, ds_buf, lanes, send.at[4], a2a_in.at[5])

    def send_back(g):
        exchange(dk_send, dtk_ref, chunk_of(g), dk_out.at[g], a2a_in.at[3])
        exchange(dv_send, dtv_ref, chunk_of(g), dv_out.at[g], a2a_in.at[4])

    x_step(2)
    y_step(0)
    y_step(1)
    sent(dk_out.at[0])
    sent(dv_out.at[0])
    send_back(1)
    z_step(0)
    y_step(2)
    z_step(1)
    z_step(2)
    wait_for(ds_buf.at[pl.ds(0, SEQ - 1)], send.at[4])
    send_back(2)

    wait_for(ds_buf, a2a_in.at[5])

    @pl.loop(0, PAIRS)
    def _(n):
        lanes = lanes_of(n, PAIR)
        q2, k2 = q_ref[:, lanes].astype(F32), k_ref[:, lanes].astype(F32)
        v2 = v_ref[:, lanes]
        g2 = ds_buf[:, :, lanes].astype(F32).reshape(PATCH, PAIR).astype(BF16)
        d_qs, d_ks, d_vs = [], [], []
        for h in range(2):
            cut = slice(h * HEAD_DIM, (h + 1) * HEAD_DIM)
            q, k = q2[:, cut], k2[:, cut]
            rq, rk = inverse_rms(q), inverse_rms(k)
            qn, kn = q * rq, k * rk
            weights = attn[2 * n + h]
            d_q, d_k, d_v = attention_back(
                weights.astype(F32), weights, q, k, qn, kn, rq, rk, qn.astype(BF16), kn.astype(BF16),
                v2[:, cut], g2[:, cut],
            )
            d_qs.append(d_q)
            d_ks.append(d_k)
            d_vs.append(d_v)
        dq_ref[:, lanes] = jnp.concatenate(d_qs, axis=1).astype(BF16)
        dk_ref[:, lanes] = jnp.concatenate(d_ks, axis=1).astype(BF16)
        dv_ref[:, lanes] = jnp.concatenate(d_vs, axis=1).astype(BF16)

        @pl.when(n == 1)
        def _():
            out_step(0)

        @pl.when(n == 3)
        def _():
            out_step(1)

    out_step(2)

    wait_for(dtk_ref, a2a_in.at[3])
    wait_for(dtv_ref, a2a_in.at[4])

    wait_for(dw_ref, out_sem)

    for sem in (tk_out.at[1], tk_out.at[2], tv_out.at[1], tv_out.at[2]):
        sent(sem)
    for sem in (dk_out.at[1], dk_out.at[2], dv_out.at[1], dv_out.at[2]):
        sent(sem)
    wait_for(weight.at[:, pl.ds(0, 2), :, pl.ds(0, 3 * COLS)], send.at[2])
    wait_for(weight.at[:, pl.ds(0, 2)], send.at[3])
    wait_for(core_in, g_send.at[0])
    wait_for(x_in, g_send.at[1])

    @pl.when(active)
    def _():
        wait_for(weight.at[pl.ds(0, NZ - 1), y, :, own_cols], send.at[0])
        wait_for(weight.at[:, 0, :, pl.ds(0, 3 * COLS)], send.at[1])
        wait_for(x_sum.at[:, 0], g_send.at[2])
        wait_for(z_in, g_send.at[3])
        wait_for(z_in, g_send.at[4])

    @pl.when(idle)
    def _():
        wait_for(x_sum, g_send.at[2])


def store(*refs):
    copies = [pltpu.make_async_copy(refs[i], refs[6 + i], refs[12].at[i]) for i in range(6)]
    for copy in copies:
        copy.start()
    for copy in copies:
        copy.wait()


def per_device(
    queries, keys_spatial, values_spatial, temporal_keys, temporal_values, tile_mask, query_weight, out_grad
):
    frame = (PATCH, WIDTH)
    blocks = (SEQ, 8, WIDTH)
    vmem = pl.BlockSpec(memory_space=pltpu.VMEM)
    smem = pl.BlockSpec(memory_space=pltpu.SMEM)
    anywhere = pl.BlockSpec(memory_space=pl.ANY)
    dma = pltpu.SemaphoreType.DMA

    def buf(*shape, kind=BF16):
        return pltpu.VMEM(shape, kind)

    results = pl.pallas_call(
        kernel,
        out_shape=(
            *(pltpu.VMEM(frame, BF16) for _ in range(3)),
            *(pltpu.VMEM(blocks, BF16) for _ in range(2)),
            pltpu.VMEM((ROWS, WIDTH), BF16),
        ),
        in_specs=[smem] + [anywhere] * 7,
        out_specs=(vmem,) * 6,
        scratch_shapes=[
            buf(*frame), buf(*frame), buf(*frame), buf(*blocks), buf(ROWS, WIDTH),
            buf(NZ, NY, ROWS, WIDTH),
            buf(PATCH, PATCH, kind=F32),
            buf(PATCH, PATCH, kind=F32),
            buf(*blocks), buf(*blocks), buf(*blocks), buf(*blocks),
            buf(*frame), buf(*frame),
            buf(HEADS, PATCH, PATCH),
            buf(*blocks), buf(*blocks), buf(*blocks), buf(*blocks),
            buf(THIRDS, NZ, NY, ROWS, CHUNK),
            buf(THIRDS, 2, NZ, ROWS, CHUNK),
            buf(THIRDS, NX - 1, 2, NZ, ROWS, HEAD_DIM),
            buf(THIRDS, 2, NZ, ROWS, HEAD_DIM),
            buf(THIRDS, NY - 1, NZ, ROWS, HEAD_DIM),
            buf(THIRDS, NZ, ROWS, HEAD_DIM),
            buf(THIRDS, NZ - 1, ROWS, HEAD_DIM),
            buf(THIRDS, ROWS, HEAD_DIM),
            dma((5,)), dma((5,)), dma((6,)), *(dma((THIRDS,)) for _ in range(9)), dma((THIRDS, NX - 1)), dma,
            dma((THIRDS,)), dma((THIRDS,)), dma((THIRDS,)), dma((THIRDS,)), dma, dma((5,)),
        ],
        compiler_params=pltpu.CompilerParams(
            collective_id=0, has_side_effects=True, vmem_limit_bytes=56 << 20
        ),
    )(
        tile_mask.reshape(2, 2),
        queries.reshape(frame),
        keys_spatial.reshape(frame),
        values_spatial.reshape(frame),
        temporal_keys.reshape(blocks),
        temporal_values.reshape(blocks),
        query_weight,
        out_grad.reshape(blocks),
    )
    d_q, d_k, d_v, d_tk, d_tv, d_w = pl.pallas_call(
        store,
        out_shape=tuple(jax.ShapeDtypeStruct(a.shape, a.dtype) for a in results),
        in_specs=[anywhere] * 6,
        out_specs=(anywhere,) * 6,
        scratch_shapes=[dma((6,))],
        compiler_params=pltpu.CompilerParams(vmem_limit_bytes=1 << 20),
    )(*results)
    whole = (1, 1, PATCH, WIDTH)
    return (*(a.reshape(whole) for a in (d_q, d_k, d_v, d_tk, d_tv)), d_w)


def solution(mesh):
    framed = P("dp", "seq", None, None)
    return jax.shard_map(
        per_device,
        mesh=mesh,
        in_specs=(framed,) * 6 + (P("seq", None), P("dp", None, "seq", None)),
        out_specs=(framed,) * 5 + (P("seq", None),),
        check_vma=False,
    )
```

```python
import math

import jax
import jax.numpy as jnp
from jax import lax
from jax.experimental import pallas as pl
from jax.experimental.pallas import tpu as pltpu
from jax.sharding import PartitionSpec as P

HEADS = 12
HEAD_DIM = 128
TILE = 128
WIDTH = HEADS * HEAD_DIM
NX, NY, NZ = 4, 4, 8
SEQ = NZ * NY
ROWS = 48
PATCH = 256
PAIR = 2 * HEAD_DIM
PAIRS = WIDTH // PAIR
CHUNK = 512
THIRDS = WIDTH // CHUNK
COLS = WIDTH // NX
SCALE = 1.0 / math.sqrt(HEAD_DIM)
SCALE2 = SCALE * math.log2(math.e)
EPS = 1e-06
MESH = pl.DeviceIdType.MESH
F32 = jnp.float32
BF16 = jnp.bfloat16


def dot(a, b, contract):
    return lax.dot_general(a, b, ((contract[:1], contract[1:]), ((), ())), preferred_element_type=F32)


def inverse_rms(a):
    return lax.rsqrt(jnp.mean(a * a, axis=-1, keepdims=True) + EPS)


def norm_back(grad, normed, inverse):
    return (inverse * SCALE) * (grad - normed * jnp.mean(grad * normed, axis=-1, keepdims=True))


def softmax(q_norm, k_norm, mask):
    exps = jnp.exp2(dot(q_norm, k_norm, (1, 1)) * SCALE2) * mask
    return exps * (1.0 / jnp.sum(exps, axis=-1, keepdims=True))


def attention_back(weights, weights_b, q, k, qn, kn, rq, rk, qn_b, kn_b, v, grad):
    d_weights = dot(grad, v, (1, 1))
    delta = jnp.sum(weights * d_weights, axis=-1, keepdims=True)
    d_scores = (weights * (d_weights - delta)).astype(BF16)
    d_v = dot(weights_b, grad, (0, 0))
    d_q = norm_back(dot(d_scores, kn_b, (1, 0)), qn, rq)
    d_k = norm_back(dot(d_scores, qn_b, (0, 0)), kn, rk)
    return d_q, d_k, d_v


def wait_for(ref, sem):
    pltpu.make_async_copy(ref, ref, sem).wait()


def kernel(
    tile_ref, q_in, k_in, v_in, tk_ref, tv_ref, w_in_ref, og_in,
    dq_ref, dk_ref, dv_ref, dtk_ref, dtv_ref, dw_ref,
    q_ref, k_ref, v_ref, og_ref, w_ref, weight, mask, tmask, spatial, k_buf, v_buf, s_buf, s_mat, d_mat, attn,
    dk_send, dv_send, ds_send, ds_buf,
    part, core_in, x_in, x_sum, y_in, y_sum, z_in, final,
    load, send, a2a_in, tk_in, tv_in, tk_out, tv_out, s_out, dk_out, dv_out, wz_in, wy_in, wx_in, wc_in,
    core_sem, x_sem, y_sem, z_sem, out_sem, g_send,
):
    d = lax.axis_index("dp")
    s = lax.axis_index("seq")
    x, c = d // 2, d % 2
    z, y = s // NY, s % NY
    sibling = {"dp": x * 2 + 1 - c}
    active = y % 2 == c
    idle = y % 2 != c

    def seq_peer(o):
        return lax.rem(s + o, SEQ)

    def x_peer(o):
        return {"dp": lax.rem(x + o, NX) * 2 + c}

    def y_peer(o):
        return {"seq": z * NY + lax.rem(y + o, NY)}

    def z_peer(o):
        return {"seq": lax.rem(z + o, NZ) * NY + y}

    def remote(src, dst, send_sem, recv_sem, device):
        pltpu.make_async_remote_copy(
            src, dst, send_sem, recv_sem, device_id=device, device_id_type=MESH
        ).start()

    def exchange(src, dst, lanes, send_sem, recv_sem):
        pltpu.make_async_copy(src.at[s, :, lanes], dst.at[s, :, lanes], recv_sem).start()

        @pl.loop(1, SEQ)
        def _(o):
            j = seq_peer(o)
            remote(src.at[j, :, lanes], dst.at[s, :, lanes], send_sem, recv_sem, {"seq": j})

    def lanes_of(n, width):
        return pl.ds(pl.multiple_of(n * width, width), width)

    own_cols = lanes_of(x, COLS)

    def chunk_of(g):
        return lanes_of(g, CHUNK)

    loads = ((w_in_ref, w_ref), (q_in, q_ref), (k_in, k_ref), (v_in, v_ref), (og_in, og_ref))
    for i, (src, dst) in enumerate(loads):
        pltpu.make_async_copy(src, dst, load.at[i]).start()

    wait_for(w_ref, load.at[0])
    weight[z, y] = w_ref[...]

    barrier = pltpu.get_barrier_semaphore()

    @pl.loop(1, SEQ)
    def _(o):
        pl.semaphore_signal(barrier, inc=1, device_id={"seq": seq_peer(o)}, device_id_type=MESH)

    @pl.loop(1, 2 * NX)
    def _(o):
        pl.semaphore_signal(barrier, inc=1, device_id={"dp": lax.rem(d + o, 2 * NX)}, device_id_type=MESH)

    ones = jnp.ones((TILE, TILE), F32)
    for a in range(2):
        for b in range(2):
            value = 1.0 if a == b else jnp.where(tile_ref[a, b] == 1, 1.0, 0.0).astype(F32)
            mask[a * TILE:(a + 1) * TILE, b * TILE:(b + 1) * TILE] = ones * value
    row = lax.broadcasted_iota(jnp.int32, (PATCH, PATCH), 0)
    col = lax.broadcasted_iota(jnp.int32, (PATCH, PATCH), 1)
    tmask[...] = jnp.where(row % 8 == col % 8, 1.0, 0.0).astype(F32)

    pl.semaphore_wait(barrier, SEQ - 1 + 2 * NX - 1)

    def cols_of(xs, g):
        return pl.ds(pl.multiple_of(xs * COLS + g * HEAD_DIM, HEAD_DIM), HEAD_DIM)

    for g in range(THIRDS):
        @pl.when(active)
        def _():
            src = weight.at[z, y, :, cols_of(x, g)]

            @pl.loop(1, NZ)
            def _(o):
                remote(src, src, send.at[0], wz_in.at[g], z_peer(o))

    exchange(tk_ref, k_buf, chunk_of(0), tk_out.at[0], tk_in.at[0])

    for i in (1, 2, 3):
        wait_for(loads[i][1], load.at[i])

    @pl.loop(0, PAIRS)
    def _(n):
        lanes = lanes_of(n, PAIR)
        q2, k2 = q_ref[:, lanes].astype(F32), k_ref[:, lanes].astype(F32)
        v2 = v_ref[:, lanes]
        outs = []
        for h in range(2):
            cut = slice(h * HEAD_DIM, (h + 1) * HEAD_DIM)
            q, k = q2[:, cut], k2[:, cut]
            qn = (q * inverse_rms(q)).astype(BF16)
            kn = (k * inverse_rms(k)).astype(BF16)
            weights = softmax(qn, kn, mask[...]).astype(BF16)
            attn[2 * n + h] = weights
            outs.append(dot(weights, v2[:, cut], (1, 0)))
        out = jnp.concatenate(outs, axis=1)
        spatial[:, :, lanes] = out.reshape(SEQ, 8, PAIR).astype(BF16)

        @pl.when(n % 2 == 1)
        def _():
            exchange(spatial, s_buf, chunk_of(n // 2), s_out.at[n // 2], a2a_in.at[1])

    def sent(sem):
        wait_for(k_buf.at[pl.ds(0, SEQ - 1), :, pl.ds(0, CHUNK)], sem)

    def send_k(g):
        exchange(tk_ref, k_buf, chunk_of(g), tk_out.at[g], tk_in.at[g])

    def send_v(g):
        exchange(tv_ref, v_buf, chunk_of(g), tv_out.at[g], tv_in.at[g])

    for g in range(THIRDS):
        @pl.when(active)
        def _():
            wait_for(weight.at[pl.ds(0, NZ - 1), y, :, cols_of(x, g)], wz_in.at[g])
            src = weight.at[:, y, :, cols_of(x, g)]

            @pl.loop(1, NY)
            def _(o):
                remote(src, src, send.at[1], wy_in.at[g], y_peer(o))

    sent(tk_out.at[0])
    send_v(0)

    for g in range(THIRDS):
        @pl.when(active)
        def _():
            wait_for(weight.at[:, 0, :, cols_of(x, g)], wy_in.at[g])

        @pl.when(idle)
        def _():
            wait_for(weight.at[:, pl.ds(0, 2), :, cols_of(x, g)], wy_in.at[g])

        for h in range(2):
            src = weight.at[:, c + 2 * h, :, cols_of(x, g)]

            @pl.loop(1, NX)
            def _(o):
                remote(src, src, send.at[2], wx_in.at[g, o - 1], x_peer(o))

            remote(src, src, send.at[3], wc_in, sibling)

    sent(s_out.at[0])
    send_k(1)
    sent(s_out.at[1])
    send_v(1)

    for g in range(THIRDS):
        for o in (1, 3, 2):
            cols = cols_of(lax.rem(x + NX - o, NX), g)
            wait_for(weight.at[:, pl.ds(0, 2), :, cols], wx_in.at[g, o - 1])
            for h in range(2):
                src = weight.at[:, c + 2 * h, :, cols]
                remote(src, src, send.at[3], wc_in, sibling)
        if g == 0:
            sent(s_out.at[2])
            send_k(2)
        if g == 1:
            sent(tv_out.at[0])
            send_v(2)

    wait_for(s_buf, a2a_in.at[1])
    for n in range(PAIRS):
        lanes = slice(n * PAIR, (n + 1) * PAIR)
        s_mat[:, lanes] = s_buf[:, :, lanes].astype(F32).reshape(PATCH, PAIR).astype(BF16)
    wait_for(weight.at[:, pl.ds(0, 2)], wc_in)
    wait_for(og_ref, load.at[4])

    def part_step(g):
        cols = d_mat[:, chunk_of(g)]

        @pl.loop(0, NZ // 2)
        def _(m):
            block = dot(s_mat[:, lanes_of(m, 2 * NY * ROWS)], cols, (0, 0))
            part[g, pl.ds(2 * m, 2)] = block.reshape(2, NY, ROWS, CHUNK).astype(BF16)

        for h in range(2):
            remote(part.at[g, :, 1 - c + 2 * h], core_in.at[g, h], g_send.at[0], core_sem.at[g], sibling)

    def x_step(g):
        wait_for(core_in.at[g], core_sem.at[g])
        for h in range(2):
            own = part[g, :, c + 2 * h].astype(F32) + core_in[g, h].astype(F32)
            part[g, :, c + 2 * h] = own.astype(BF16)

            @pl.loop(1, NX)
            def _(o):
                to = lax.rem(x + o, NX)
                remote(
                    part.at[g, :, c + 2 * h, :, lanes_of(to, HEAD_DIM)], x_in.at[g, o - 1, h],
                    g_send.at[1], x_sem.at[g], x_peer(o),
                )

    def y_step(g):
        wait_for(x_in.at[g], x_sem.at[g])
        for h in range(2):
            total = part[g, :, c + 2 * h, :, lanes_of(x, HEAD_DIM)].astype(F32)
            for o in range(NX - 1):
                total = total + x_in[g, o, h].astype(F32)
            x_sum[g, h] = total.astype(BF16)
            owner = c + 2 * h

            @pl.when(y != owner)
            def _():
                away = lax.rem(y - owner + NY, NY)
                remote(x_sum.at[g, h], y_in.at[g, away - 1], g_send.at[2], y_sem.at[g], {"seq": z * NY + owner})

    def z_step(g):
        @pl.when(active)
        def _():
            wait_for(y_in.at[g], y_sem.at[g])
            total = x_sum[g, y // 2].astype(F32)
            for o in range(NY - 1):
                total = total + y_in[g, o].astype(F32)
            y_sum[g] = total.astype(BF16)

            @pl.loop(1, NZ)
            def _(o):
                remote(
                    y_sum.at[g, lax.rem(z + o, NZ)], z_in.at[g, o - 1], g_send.at[3], z_sem.at[g], z_peer(o)
                )

    def out_step(g):
        @pl.when(active)
        def _():
            wait_for(z_in.at[g], z_sem.at[g])
            total = y_sum[g, z].astype(F32)
            for o in range(NZ - 1):
                total = total + z_in[g, o].astype(F32)
            final[g] = total.astype(BF16)
            dst = dw_ref.at[:, pl.ds(pl.multiple_of(g * CHUNK + x * HEAD_DIM, HEAD_DIM), HEAD_DIM)]
            pltpu.make_async_copy(final.at[g], dst, out_sem).start()

            @pl.loop(1, 2 * NX)
            def _(o):
                remote(final.at[g], dst, g_send.at[4], out_sem, {"dp": lax.rem(d + o, 2 * NX)})

    @pl.loop(0, PAIRS)
    def _(n):
        lanes = lanes_of(n, PAIR)

        @pl.when(n % 2 == 0)
        def _():
            g = n // 2
            wait_for(k_buf.at[:, :, chunk_of(g)], tk_in.at[g])
            wait_for(v_buf.at[:, :, chunk_of(g)], tv_in.at[g])

        rows = weight[:, :, :, lanes].reshape(WIDTH, PAIR)
        q2 = dot(s_mat[...], rows, (1, 0)).astype(BF16).astype(F32)
        k2 = k_buf[:, :, lanes].astype(F32).reshape(PATCH, PAIR)
        v2 = v_buf[:, :, lanes].astype(F32).reshape(PATCH, PAIR).astype(BF16)
        g2 = og_ref[:, :, lanes].astype(F32).reshape(PATCH, PAIR).astype(BF16)
        d_qs, d_ks, d_vs = [], [], []
        for h in range(2):
            cut = slice(h * HEAD_DIM, (h + 1) * HEAD_DIM)
            q, k = q2[:, cut], k2[:, cut]
            rq, rk = inverse_rms(q), inverse_rms(k)
            qn, kn = q * rq, k * rk
            qn_b, kn_b = qn.astype(BF16), kn.astype(BF16)
            weights = softmax(qn_b, kn_b, tmask[...])
            d_q, d_k, d_v = attention_back(
                weights, weights.astype(BF16), q, k, qn, kn, rq, rk, qn_b, kn_b, v2[:, cut], g2[:, cut]
            )
            d_qs.append(d_q)
            d_ks.append(d_k)
            d_vs.append(d_v)
        d_mat[:, lanes] = jnp.concatenate(d_qs, axis=1).astype(BF16)
        dk_send[:, :, lanes] = jnp.concatenate(d_ks, axis=1).reshape(SEQ, 8, PAIR).astype(BF16)
        dv_send[:, :, lanes] = jnp.concatenate(d_vs, axis=1).reshape(SEQ, 8, PAIR).astype(BF16)

        @pl.when(n % 2 == 1)
        def _():
            part_step(n // 2)

        @pl.when(n == 3)
        def _():
            x_step(0)

        @pl.when(n == 5)
        def _():
            x_step(1)

        @pl.when(n == 1)
        def _():
            first = pl.ds(0, CHUNK)
            exchange(dk_send, dtk_ref, first, dk_out.at[0], a2a_in.at[3])
            exchange(dv_send, dtv_ref, first, dv_out.at[0], a2a_in.at[4])

    x_step(2)

    @pl.loop(0, NZ // 2)
    def _(m):
        rows = weight[pl.ds(2 * m, 2)].reshape(2 * NY * ROWS, WIDTH)
        out = dot(d_mat[...], rows, (1, 1))
        lanes = lanes_of(m, 2 * NY * ROWS)
        ds_send[:, :, lanes] = out.reshape(SEQ, 8, 2 * NY * ROWS).astype(BF16)
        exchange(ds_send, ds_buf, lanes, send.at[4], a2a_in.at[5])

    def send_back(g):
        exchange(dk_send, dtk_ref, chunk_of(g), dk_out.at[g], a2a_in.at[3])
        exchange(dv_send, dtv_ref, chunk_of(g), dv_out.at[g], a2a_in.at[4])

    y_step(0)
    y_step(1)
    sent(dk_out.at[0])
    sent(dv_out.at[0])
    send_back(1)
    z_step(0)
    y_step(2)
    z_step(1)
    z_step(2)
    wait_for(ds_buf.at[pl.ds(0, SEQ - 1)], send.at[4])
    send_back(2)

    wait_for(ds_buf, a2a_in.at[5])

    @pl.loop(0, PAIRS)
    def _(n):
        lanes = lanes_of(n, PAIR)
        q2, k2 = q_ref[:, lanes].astype(F32), k_ref[:, lanes].astype(F32)
        v2 = v_ref[:, lanes]
        g2 = ds_buf[:, :, lanes].astype(F32).reshape(PATCH, PAIR).astype(BF16)
        d_qs, d_ks, d_vs = [], [], []
        for h in range(2):
            cut = slice(h * HEAD_DIM, (h + 1) * HEAD_DIM)
            q, k = q2[:, cut], k2[:, cut]
            rq, rk = inverse_rms(q), inverse_rms(k)
            qn, kn = q * rq, k * rk
            weights = attn[2 * n + h]
            d_q, d_k, d_v = attention_back(
                weights.astype(F32), weights, q, k, qn, kn, rq, rk, qn.astype(BF16), kn.astype(BF16),
                v2[:, cut], g2[:, cut],
            )
            d_qs.append(d_q)
            d_ks.append(d_k)
            d_vs.append(d_v)
        dq_ref[:, lanes] = jnp.concatenate(d_qs, axis=1).astype(BF16)
        dk_ref[:, lanes] = jnp.concatenate(d_ks, axis=1).astype(BF16)
        dv_ref[:, lanes] = jnp.concatenate(d_vs, axis=1).astype(BF16)

        @pl.when(n == 1)
        def _():
            out_step(0)

        @pl.when(n == 3)
        def _():
            out_step(1)

    out_step(2)

    wait_for(dtk_ref, a2a_in.at[3])
    wait_for(dtv_ref, a2a_in.at[4])

    wait_for(dw_ref, out_sem)

    for sem in (tk_out.at[1], tk_out.at[2], tv_out.at[1], tv_out.at[2]):
        sent(sem)
    for sem in (dk_out.at[1], dk_out.at[2], dv_out.at[1], dv_out.at[2]):
        sent(sem)
    wait_for(weight.at[:, pl.ds(0, 2), :, pl.ds(0, 3 * COLS)], send.at[2])
    wait_for(weight.at[:, pl.ds(0, 2)], send.at[3])
    wait_for(core_in, g_send.at[0])
    wait_for(x_in, g_send.at[1])

    @pl.when(active)
    def _():
        wait_for(weight.at[pl.ds(0, NZ - 1), y, :, own_cols], send.at[0])
        wait_for(weight.at[:, 0, :, pl.ds(0, 3 * COLS)], send.at[1])
        wait_for(x_sum.at[:, 0], g_send.at[2])
        wait_for(z_in, g_send.at[3])
        wait_for(z_in, g_send.at[4])

    @pl.when(idle)
    def _():
        wait_for(x_sum, g_send.at[2])


def store(*refs):
    copies = [pltpu.make_async_copy(refs[i], refs[6 + i], refs[12].at[i]) for i in range(6)]
    for copy in copies:
        copy.start()
    for copy in copies:
        copy.wait()


def per_device(
    queries, keys_spatial, values_spatial, temporal_keys, temporal_values, tile_mask, query_weight, out_grad
):
    frame = (PATCH, WIDTH)
    blocks = (SEQ, 8, WIDTH)
    vmem = pl.BlockSpec(memory_space=pltpu.VMEM)
    smem = pl.BlockSpec(memory_space=pltpu.SMEM)
    anywhere = pl.BlockSpec(memory_space=pl.ANY)
    dma = pltpu.SemaphoreType.DMA

    def buf(*shape, kind=BF16):
        return pltpu.VMEM(shape, kind)

    results = pl.pallas_call(
        kernel,
        out_shape=(
            *(pltpu.VMEM(frame, BF16) for _ in range(3)),
            *(pltpu.VMEM(blocks, BF16) for _ in range(2)),
            pltpu.VMEM((ROWS, WIDTH), BF16),
        ),
        in_specs=[smem] + [anywhere] * 7,
        out_specs=(vmem,) * 6,
        scratch_shapes=[
            buf(*frame), buf(*frame), buf(*frame), buf(*blocks), buf(ROWS, WIDTH),
            buf(NZ, NY, ROWS, WIDTH),
            buf(PATCH, PATCH, kind=F32),
            buf(PATCH, PATCH, kind=F32),
            buf(*blocks), buf(*blocks), buf(*blocks), buf(*blocks),
            buf(*frame), buf(*frame),
            buf(HEADS, PATCH, PATCH),
            buf(*blocks), buf(*blocks), buf(*blocks), buf(*blocks),
            buf(THIRDS, NZ, NY, ROWS, CHUNK),
            buf(THIRDS, 2, NZ, ROWS, CHUNK),
            buf(THIRDS, NX - 1, 2, NZ, ROWS, HEAD_DIM),
            buf(THIRDS, 2, NZ, ROWS, HEAD_DIM),
            buf(THIRDS, NY - 1, NZ, ROWS, HEAD_DIM),
            buf(THIRDS, NZ, ROWS, HEAD_DIM),
            buf(THIRDS, NZ - 1, ROWS, HEAD_DIM),
            buf(THIRDS, ROWS, HEAD_DIM),
            dma((5,)), dma((5,)), dma((6,)), *(dma((THIRDS,)) for _ in range(9)), dma((THIRDS, NX - 1)), dma,
            dma((THIRDS,)), dma((THIRDS,)), dma((THIRDS,)), dma((THIRDS,)), dma, dma((5,)),
        ],
        compiler_params=pltpu.CompilerParams(
            collective_id=0, has_side_effects=True, vmem_limit_bytes=56 << 20
        ),
    )(
        tile_mask.reshape(2, 2),
        queries.reshape(frame),
        keys_spatial.reshape(frame),
        values_spatial.reshape(frame),
        temporal_keys.reshape(blocks),
        temporal_values.reshape(blocks),
        query_weight,
        out_grad.reshape(blocks),
    )
    d_q, d_k, d_v, d_tk, d_tv, d_w = pl.pallas_call(
        store,
        out_shape=tuple(jax.ShapeDtypeStruct(a.shape, a.dtype) for a in results),
        in_specs=[anywhere] * 6,
        out_specs=(anywhere,) * 6,
        scratch_shapes=[dma((6,))],
        compiler_params=pltpu.CompilerParams(vmem_limit_bytes=1 << 20),
    )(*results)
    whole = (1, 1, PATCH, WIDTH)
    return (*(a.reshape(whole) for a in (d_q, d_k, d_v, d_tk, d_tv)), d_w)


def solution(mesh):
    framed = P("dp", "seq", None, None)
    return jax.shard_map(
        per_device,
        mesh=mesh,
        in_specs=(framed,) * 6 + (P("seq", None), P("dp", None, "seq", None)),
        out_specs=(framed,) * 5 + (P("seq", None),),
        check_vma=False,
    )
```
